512 devices in a mesh: row: 32 (over y, x_lo, core), col: 16 (over x_hi, z).
Axes of the slice: x: 4 (x_hi: 2, x_lo: 2; x = x_hi * 2 + x_lo), y: 8, z: 8, core: 2. Of those that a mesh axis runs over, the one named last changes fastest.
Arguments:
- picture_encoder_output: bfloat16 [98304, 1152], P(('row', 'col')), may hold values from -0.59765625 to 0.59765625
- caption_encoder_output: bfloat16 [98304, 1152], P(('row', 'col')), may hold values from -0.59765625 to 0.59765625
- softness_factor_exponent: float32 [], replicated, may hold values from 2.7 to 3.7
- logit_offset_term: float32 [], replicated, may hold values from -5 to -2
Outputs:
- image_grad: float32 [98304, 1152], P(('row', 'col'))
- text_grad: float32 [98304, 1152], P(('row', 'col'))
The draws below stay inside these ranges and needn't reach their ends.
All inputs are finite; a program needn't handle non-finite values.
Results may differ from the reference program's by a relative error of at most 0.008.
Values may be sent and summed in bfloat16 or wider, within the bound.
A program may use at most 64 MiB of HBM per device.

```python
import jax
import jax.numpy as jnp
from jax import lax

EMBED = 1152
ROWS_DEV = 192
SPAN_ROW = 8
SPAN_COL = 4
BATCH = 98304
N_ROW = 32
N_COL = 16


def block_levels(rng, dims, cuts, least, high):
    level = 1.0
    for dim, shards_of in cuts:
        steps = jax.random.uniform(jax.random.fold_in(jax.random.fold_in(rng, 6), dim), (shards_of,), jnp.float32, least / len(cuts), high / len(cuts))
        level = level * jnp.repeat(jnp.exp(steps), dims[dim] // shards_of).reshape((-1,) + (1,) * (len(dims) - 1 - dim))
    return level


def noise(rng, shape, spread, reach, split=(), held_as=jnp.bfloat16):
    drawn = spread * jax.random.normal(rng, shape, jnp.float32)
    if split:
        drawn = drawn * block_levels(rng, shape, split, -0.22, 0.18)
    return jnp.clip(drawn, -reach, reach).astype(held_as)


def setup_inputs(seed: int = 0) -> dict:
    seeds = jax.random.split(jax.random.key(seed), 5)
    return {
        "picture_encoder_output": noise(seeds[0], (BATCH, EMBED), 0.1, 0.59765625, ((0, 512),)),
        "caption_encoder_output": noise(seeds[1], (BATCH, EMBED), 0.1, 0.59765625, ((0, 512),)),
        "softness_factor_exponent": jnp.clip(jax.random.uniform(seeds[2], (), jnp.float32, 2.7, 3.7), 2.7, 3.7),
        "logit_offset_term": jnp.clip(jax.random.uniform(seeds[3], (), jnp.float32, -5.0, -2.0), -5.0, -2.0),
    }


eps_norm = 1e-06

def unit_rows(feature):
    values = feature.astype(jnp.float32)
    inverse = lax.rsqrt(lax.optimization_barrier(jnp.sum(values * values, axis=-1, keepdims=True)) + eps_norm)
    return (values * inverse, inverse)

def unit_back(unit, inverse, direction):
    along = lax.optimization_barrier(jnp.sum(unit * direction, axis=-1, keepdims=True))
    return inverse * (direction - unit * along)

def reference(picture_encoder_output, caption_encoder_output, softness_factor_exponent, logit_offset_term):
    img_unit, img_inv = unit_rows(picture_encoder_output)
    txt_unit, text_inverse_norm = unit_rows(caption_encoder_output)
    img_half = img_unit.astype(jnp.bfloat16)
    txt_half = txt_unit.astype(jnp.bfloat16)
    trained_softness_factor = jnp.exp(softness_factor_exponent.astype(jnp.float32))
    images = img_half.astype(jnp.float32).reshape(N_ROW, N_COL, ROWS_DEV, EMBED)
    texts = txt_half.astype(jnp.float32).reshape(N_ROW, N_COL, ROWS_DEV, EMBED)
    diagonal = jnp.eye(ROWS_DEV, dtype=jnp.float32)

    def meet(img_block, match_target_sign):
        matched_cosine_scores = jnp.einsum('abie,abje->abij', img_block, texts)
        matched_loss_multipliers = (trained_softness_factor * (jax.nn.sigmoid(trained_softness_factor * matched_cosine_scores + logit_offset_term) - match_target_sign)).astype(jnp.bfloat16)
        matched_loss_multipliers = matched_loss_multipliers.astype(jnp.float32)
        img_part = jnp.einsum('abij,abje->abie', matched_loss_multipliers, texts)
        txt_part = jnp.einsum('abij,abie->abje', matched_loss_multipliers, img_block)
        return (img_part, txt_part)
    img_dir = jnp.zeros((N_ROW, N_COL, ROWS_DEV, EMBED), jnp.float32)
    txt_dir = jnp.zeros((N_ROW, N_COL, ROWS_DEV, EMBED), jnp.float32)
    for offset in range(SPAN_ROW):
        match_target_sign = diagonal if offset == 0 else 0.0
        img_part, txt_part = meet(jnp.roll(images, -offset, axis=0), match_target_sign)
        img_dir = img_dir + jnp.roll(img_part, offset, axis=0)
        txt_dir = txt_dir + txt_part
    for offset in range(1, SPAN_COL):
        img_part, txt_part = meet(jnp.roll(images, -offset, axis=1), 0.0)
        img_dir = img_dir + jnp.roll(img_part, offset, axis=1)
        txt_dir = txt_dir + txt_part
    img_dir = img_dir.reshape(BATCH, EMBED)
    txt_dir = txt_dir.reshape(BATCH, EMBED)
    return (unit_back(img_unit, img_inv, img_dir), unit_back(txt_unit, text_inverse_norm, txt_dir))
```

```python
import functools

import jax
import jax.numpy as jnp
from jax import lax
from jax.experimental import pallas as pl
from jax.experimental.pallas import tpu as pltpu
from jax.sharding import PartitionSpec as P

MESH = pl.DeviceIdType.MESH
eps_norm = 1e-06

OWN, COL = 0, 7
CHUNKS = 2


def kernel(
    n_row, n_col, scale_ref, bias_ref, txt_ref, img_ref, img_out, txt_out, raw, buf, acc, inv, send_sem, recv_sem, load_sem
):
    rows, width = txt_ref.shape
    part = rows // CHUNKS
    row, col = lax.axis_index("row"), lax.axis_index("col")
    core = lax.rem(row, 2)
    half = lax.rem(row // 2, 2)

    def at_row(offset):
        return (lax.rem(row + offset + n_row, n_row), col)

    def at_col(offset):
        return (row, lax.rem(col + offset + n_col, n_col))

    sibling = at_row(1 - 2 * core)
    partner = at_row(2 - 4 * half)
    across = at_row(6 * core - 3)

    barrier = pltpu.get_barrier_semaphore()
    peers = (at_row(4), at_row(-4), sibling, partner, across, at_col(1), at_col(-1))
    for peer in peers:
        pl.semaphore_signal(barrier, inc=1, device_id=peer, device_id_type=MESH)

    loads = [pltpu.make_async_copy(ref, raw.at[d], load_sem.at[d]) for d, ref in enumerate((txt_ref, img_ref))]
    for load in loads:
        load.start()
    for load in loads:
        load.wait()

    def normalise(d, c):
        span = pl.ds(c * part, part)
        values = raw[d, span, :].astype(jnp.float32)
        inverse = lax.rsqrt(jnp.sum(values * values, axis=-1, keepdims=True) + eps_norm)
        inv[d, span, :] = inverse
        buf[d, OWN, span, :] = (values * inverse).astype(jnp.bfloat16)

    for c in range(CHUNKS):
        for d in range(2):
            normalise(d, c)

    pl.semaphore_wait(barrier, len(peers))

    def copy(d, number, source, slot, c, target):
        span = pl.ds(c * part, part)
        return pltpu.make_async_remote_copy(
            src_ref=buf.at[d, source, span],
            dst_ref=buf.at[d, slot, span],
            send_sem=send_sem.at[d, number, c],
            recv_sem=recv_sem.at[d, slot, c],
            device_id=target,
            device_id_type=MESH,
        )

    def place(d):
        sign = 1 - 2 * d
        return sign, jnp.where(d == 0, half, 1 - half), jnp.where(d == 0, core, 1 - core)

    def first_sends(d, c):
        sign, h, e = place(d)
        copy(d, 0, OWN, COL + 1, c, at_col(sign)).start()
        copy(d, 3, OWN, 4, c, at_row(4 * sign)).start()

        @pl.when(h == 0)
        def _():
            copy(d, 5, OWN, 2, c, partner).start()

        @pl.when(e == 0)
        def _():
            copy(d, 6, OWN, 1, c, sibling).start()

    def arrived(d, slot, c):
        copy(d, 0, OWN, slot, c, sibling).wait_recv()

    def pass_on(d, slot, c):
        arrived(d, slot, c)
        sign, h, e = place(d)
        if slot == COL + 1 or slot == COL + 2:
            copy(d, slot - COL, slot, slot + 1, c, at_col(sign)).start()
        elif slot == 4:

            @pl.when(h == 1)
            def _():
                copy(d, 5, 4, 2, c, partner).start()

            @pl.when(e == 1)
            def _():
                copy(d, 6, 4, 7, c, across).start()

            copy(d, 8, 4, 5 - 2 * e, c, sibling).start()
        elif slot == 2:
            copy(d, 4, 2, 6, c, at_row(4 * sign)).start()
            copy(d, 7, 2, 3 - 2 * e, c, sibling).start()
        elif slot == 6:
            copy(d, 9, 6, 7 - 2 * e, c, sibling).start()

    for c in range(CHUNKS):
        for d in range(2):
            first_sends(d, c)

    scale = jnp.exp(jnp.full((1, rows), scale_ref[0, 0], jnp.float32))
    bias = bias_ref[0, 0]

    def meet(d, slot, on_diagonal=False):
        other = buf[d, slot]
        cosines = lax.dot_general(
            buf[1 - d, OWN], other, (((1,), (1,)), ((), ())), preferred_element_type=jnp.float32
        )
        chance = jax.nn.sigmoid(scale * cosines + bias)
        if on_diagonal:
            across_rows = lax.broadcasted_iota(jnp.int32, (rows, rows), 0)
            across_cols = lax.broadcasted_iota(jnp.int32, (rows, rows), 1)
            chance = chance - jnp.where(across_rows == across_cols, 1.0, 0.0)
        weights = (scale * chance).astype(jnp.bfloat16)
        term = jnp.dot(weights, other, preferred_element_type=jnp.float32)
        acc[d] = term if on_diagonal else acc[d] + term

    def meet_both(slot, on_diagonal=False):
        @pl.loop(0, 2)
        def _(d):
            meet(d, slot, on_diagonal)

    def both(slot, c):
        for d in range(2):
            pass_on(d, slot, c)

    def land(slot):
        for c in range(CHUNKS):
            for d in range(2):
                arrived(d, slot, c)

    meet_both(OWN, True)
    for c in range(CHUNKS):
        both(4, c)
        both(COL + 1, c)
    for c in range(CHUNKS):
        pass_on(1 - half, 2, c)
    meet_both(4)
    both(COL + 2, 0)
    pass_on(half, 2, 0)
    meet_both(COL + 1)
    pass_on(half, 2, 1)
    both(COL + 2, 1)
    land(1)
    meet_both(1)
    meet_both(2)
    land(3)
    meet_both(3)
    meet_both(COL + 2)
    both(6, 0)
    both(6, 1)
    land(5)
    meet_both(5)
    meet_both(6)
    land(7)
    meet_both(7)
    land(COL + 3)
    meet_both(COL + 3)

    for d, out in ((0, img_out), (1, txt_out)):
        inverse = inv[1 - d]
        unit = raw[1 - d].astype(jnp.float32) * inverse
        direction = acc[d]
        along = jnp.sum(unit * direction, axis=-1, keepdims=True)
        out[...] = inverse * (direction - unit * along)

    for d in range(2):
        for number in range(10):
            for c in range(CHUNKS):
                copy(d, number, OWN, 1, c, sibling).wait_send()


def on_device(n_row, n_col, picture, caption, scale_exponent, offset):
    rows, width = picture.shape
    scalar = pl.BlockSpec(memory_space=pltpu.SMEM)
    whole = pl.BlockSpec(memory_space=pl.ANY)
    out = jax.ShapeDtypeStruct((rows, width), jnp.float32)
    return pl.pallas_call(
        functools.partial(kernel, n_row, n_col),
        out_shape=(out, out),
        in_specs=[scalar, scalar, whole, whole],
        out_specs=[pl.BlockSpec(memory_space=pltpu.VMEM)] * 2,
        scratch_shapes=[
            pltpu.VMEM((2, rows, width), jnp.bfloat16),
            pltpu.VMEM((2, 11, rows, width), jnp.bfloat16),
            pltpu.VMEM((2, rows, width), jnp.float32),
            pltpu.VMEM((2, rows, 1), jnp.float32),
            pltpu.SemaphoreType.DMA((2, 10, CHUNKS)),
            pltpu.SemaphoreType.DMA((2, 11, CHUNKS)),
            pltpu.SemaphoreType.DMA((2,)),
        ],
        compiler_params=pltpu.CompilerParams(
            collective_id=0, has_side_effects=True, vmem_limit_bytes=48 << 20
        ),
    )(scale_exponent.reshape(1, 1), offset.reshape(1, 1), caption, picture)


def solution(mesh):
    return jax.shard_map(
        functools.partial(on_device, mesh.shape["row"], mesh.shape["col"]),
        mesh=mesh,
        in_specs=(P(("row", "col"), None), P(("row", "col"), None), P(), P()),
        out_specs=(P(("row", "col"), None), P(("row", "col"), None)),
        check_vma=False,
    )
```

```python
import functools

import jax
import jax.numpy as jnp
from jax import lax
from jax.experimental import pallas as pl
from jax.experimental.pallas import tpu as pltpu
from jax.sharding import PartitionSpec as P

MESH = pl.DeviceIdType.MESH
eps_norm = 1e-06

OWN, COL, VIA = 0, 7, 11
CHUNKS = 2


def kernel(
    n_row, n_col, scale_ref, bias_ref, txt_ref, img_ref, img_out, txt_out, raw, buf, acc, inv, send_sem, recv_sem, load_sem
):
    rows, width = txt_ref.shape
    part = rows // CHUNKS
    row, col = lax.axis_index("row"), lax.axis_index("col")
    core = lax.rem(row, 2)
    half = lax.rem(row // 2, 2)

    def at(row_offset, col_offset):
        return (lax.rem(row + row_offset + n_row, n_row), lax.rem(col + col_offset + n_col, n_col))

    def at_row(offset):
        return at(offset, 0)

    def at_col(offset):
        return at(0, offset)

    depth = n_col // 2
    level = lax.rem(col, depth)
    beside = 2 - 4 * half
    sibling = at_row(1 - 2 * core)
    partner = at_row(beside)
    across = at_row(6 * core - 3)
    turn = at(
        jnp.where(jnp.logical_or(level == 0, level == depth - 1), beside, 0),
        jnp.where(level == depth - 1, 1, jnp.where(level == 0, -1, depth)),
    )

    barrier = pltpu.get_barrier_semaphore()
    peers = (at_row(4), at_row(-4), sibling, partner, across, at_col(1), at_col(-1), turn)
    for peer in peers:
        pl.semaphore_signal(barrier, inc=1, device_id=peer, device_id_type=MESH)

    loads = [pltpu.make_async_copy(ref, raw.at[d], load_sem.at[d]) for d, ref in enumerate((txt_ref, img_ref))]
    for load in loads:
        load.start()
    for load in loads:
        load.wait()

    def normalise(d, c):
        span = pl.ds(c * part, part)
        values = raw[d, span, :].astype(jnp.float32)
        inverse = lax.rsqrt(jnp.sum(values * values, axis=-1, keepdims=True) + eps_norm)
        inv[d, span, :] = inverse
        buf[d, OWN, span, :] = (values * inverse).astype(jnp.bfloat16)

    for c in range(CHUNKS):
        for d in range(2):
            normalise(d, c)

    pl.semaphore_wait(barrier, len(peers))

    def copy(d, number, source, slot, c, target):
        span = pl.ds(c * part, part)
        return pltpu.make_async_remote_copy(
            src_ref=buf.at[d, source, span],
            dst_ref=buf.at[d, slot, span],
            send_sem=send_sem.at[d, number, c],
            recv_sem=recv_sem.at[d, slot, c],
            device_id=target,
            device_id_type=MESH,
        )

    def when(*conditions):
        return pl.when(functools.reduce(jnp.logical_and, conditions))

    places = []
    for d in range(2):
        z = level if d == 0 else depth - 1 - level
        places.append((1 - 2 * d, half if d == 0 else 1 - half, core if d == 0 else 1 - core, z == depth - 1, z == 0))

    def first_sends(d, c):
        sign, h, e, last, _ = places[d]
        copy(d, 3, OWN, 4, c, at_row(4 * sign)).start()

        @when(jnp.logical_not(last), h == 0)
        def _():
            copy(d, 5, OWN, 2, c, partner).start()

        @when(jnp.logical_not(last))
        def _():
            copy(d, 0, OWN, COL + 1, c, at_col(sign)).start()

        @when(e == 0)
        def _():
            copy(d, 6, OWN, 1, c, sibling).start()

    def arrived(d, slot, c):
        copy(d, 0, OWN, slot, c, sibling).wait_recv()

    def pass_on(d, slot, c):
        arrived(d, slot, c)
        sign, h, e, last, _ = places[d]
        if slot == COL + 1 or slot == COL + 2:
            copy(d, slot - COL, slot, slot + 1, c, at_col(sign)).start()
        elif slot == VIA:
            copy(d, 0, VIA, COL + 1, c, turn).start()
            copy(d, 10, VIA, 2, c, at_row(4 * sign)).start()
        elif slot == 4:

            @when(h == 1, jnp.logical_not(last))
            def _():
                copy(d, 5, 4, 2, c, partner).start()

            @when(e == 1)
            def _():
                copy(d, 6, 4, 7, c, across).start()

            copy(d, 8, 4, 5 - 2 * e, c, sibling).start()
        elif slot == 2:

            @when(h == 1, last)
            def _():
                copy(d, 0, 2, COL + 1, c, turn).start()

            copy(d, 4, 2, 6, c, at_row(4 * sign)).start()
            copy(d, 7, 2, 3 - 2 * e, c, sibling).start()
        elif slot == 6:
            copy(d, 9, 6, 7 - 2 * e, c, sibling).start()

    for c in range(CHUNKS):
        for d in range(2):

            @pl.when(places[d][3])
            def _(d=d, c=c):
                copy(d, 5, OWN, jnp.where(places[d][1] == 0, 2, VIA), c, partner).start()

    for c in range(CHUNKS):
        for d in range(2):
            first_sends(d, c)

    scale = jnp.exp(jnp.full((1, rows), scale_ref[0, 0], jnp.float32))
    bias = bias_ref[0, 0]

    def meet(d, slot, on_diagonal=False):
        other = buf[d, slot]
        cosines = lax.dot_general(
            buf[1 - d, OWN], other, (((1,), (1,)), ((), ())), preferred_element_type=jnp.float32
        )
        chance = jax.nn.sigmoid(scale * cosines + bias)
        if on_diagonal:
            across_rows = lax.broadcasted_iota(jnp.int32, (rows, rows), 0)
            across_cols = lax.broadcasted_iota(jnp.int32, (rows, rows), 1)
            chance = chance - jnp.where(across_rows == across_cols, 1.0, 0.0)
        weights = (scale * chance).astype(jnp.bfloat16)
        term = jnp.dot(weights, other, preferred_element_type=jnp.float32)
        acc[d] = term if on_diagonal else acc[d] + term

    def meet_both(slot, on_diagonal=False):
        @pl.loop(0, 2)
        def _(d):
            meet(d, slot, on_diagonal)

    def land(slot):
        for c in range(CHUNKS):
            for d in range(2):
                arrived(d, slot, c)

    def pass_if(condition, d, slot, c):
        @pl.when(condition)
        def _():
            pass_on(d, slot, c)

    meet_both(OWN, True)
    for c in range(CHUNKS):
        for d in range(2):
            _, h, e, last, fresh = places[d]
            inner = jnp.logical_not(jnp.logical_or(last, fresh))
            pass_if(jnp.logical_and(last, h == 0), d, VIA, c)
            pass_if(jnp.logical_and(last, h == 1), d, 2, c)
            pass_on(d, 4, c)
            pass_if(inner, d, COL + 1, c)
            pass_if(jnp.logical_and(inner, h == 1), d, 2, c)
    for c in range(CHUNKS):
        for d in range(2):
            pass_if(places[d][3], d, COL + 1, c)
    meet_both(4)
    for c in range(CHUNKS):
        for d in range(2):
            pass_if(places[d][4], d, COL + 1, c)
        for d in range(2):
            pass_if(jnp.logical_not(places[d][4]), d, COL + 2, c)
        for d in range(2):
            _, h, e, last, fresh = places[d]
            pass_if(jnp.logical_or(h == 0, fresh), d, 2, c)
            pass_if(jnp.logical_and(h == 1, jnp.logical_not(fresh)), d, 6, c)
    meet_both(COL + 1)
    for c in range(CHUNKS):
        for d in range(2):
            pass_if(places[d][4], d, 6, c)
            pass_if(places[d][4], d, COL + 2, c)
        for d in range(2):
            _, h, e, last, fresh = places[d]
            pass_if(jnp.logical_and(h == 0, jnp.logical_not(fresh)), d, 6, c)
        if c == 0:
            land(1)
            meet_both(1)
            meet_both(2)
            land(3)
            meet_both(3)
    meet_both(COL + 2)
    meet_both(6)
    land(5)
    meet_both(5)
    land(7)
    meet_both(7)
    land(COL + 3)
    meet_both(COL + 3)

    for d, out in ((0, img_out), (1, txt_out)):
        inverse = inv[1 - d]
        unit = raw[1 - d].astype(jnp.float32) * inverse
        direction = acc[d]
        along = jnp.sum(unit * direction, axis=-1, keepdims=True)
        out[...] = inverse * (direction - unit * along)

    for d in range(2):
        for number in range(10):
            for c in range(CHUNKS):
                copy(d, number, OWN, 1, c, sibling).wait_send()
        for c in range(CHUNKS):

            @when(places[d][3], places[d][1] == 0)
            def _(d=d, c=c):
                copy(d, 10, OWN, 1, c, sibling).wait_send()


def on_device(n_row, n_col, picture, caption, scale_exponent, offset):
    rows, width = picture.shape
    scalar = pl.BlockSpec(memory_space=pltpu.SMEM)
    whole = pl.BlockSpec(memory_space=pltpu.HBM)
    out = jax.ShapeDtypeStruct((rows, width), jnp.float32)
    return pl.pallas_call(
        functools.partial(kernel, n_row, n_col),
        out_shape=(out, out),
        in_specs=[scalar, scalar, whole, whole],
        out_specs=[pl.BlockSpec(memory_space=pltpu.VMEM)] * 2,
        scratch_shapes=[
            pltpu.VMEM((2, rows, width), jnp.bfloat16),
            pltpu.VMEM((2, 12, rows, width), jnp.bfloat16),
            pltpu.VMEM((2, rows, width), jnp.float32),
            pltpu.VMEM((2, rows, 1), jnp.float32),
            pltpu.SemaphoreType.DMA((2, 11, CHUNKS)),
            pltpu.SemaphoreType.DMA((2, 12, CHUNKS)),
            pltpu.SemaphoreType.DMA((2,)),
        ],
        compiler_params=pltpu.CompilerParams(
            collective_id=0, has_side_effects=True, vmem_limit_bytes=48 << 20
        ),
    )(scale_exponent.reshape(1, 1), offset.reshape(1, 1), caption, picture)


def solution(mesh):
    return jax.shard_map(
        functools.partial(on_device, mesh.shape["row"], mesh.shape["col"]),
        mesh=mesh,
        in_specs=(P(("row", "col"), None), P(("row", "col"), None), P(), P()),
        out_specs=(P(("row", "col"), None), P(("row", "col"), None)),
        check_vma=False,
    )
```

```python
import functools

import jax
import jax.numpy as jnp
from jax import lax
from jax.experimental import pallas as pl
from jax.experimental.pallas import tpu as pltpu
from jax.sharding import PartitionSpec as P

MESH = pl.DeviceIdType.MESH
eps_norm = 1e-06

OWN, COL, VIA = 0, 7, 11
CHUNKS = 2


def kernel(
    n_row, n_col, scale_ref, bias_ref, txt_ref, img_ref, img_out, txt_out, raw, buf, acc, inv, send_sem, recv_sem, load_sem
):
    rows, width = txt_ref.shape
    part = rows // CHUNKS
    row, col = lax.axis_index("row"), lax.axis_index("col")
    core = lax.rem(row, 2)
    half = lax.rem(row // 2, 2)

    def at(row_offset, col_offset):
        return (lax.rem(row + row_offset + n_row, n_row), lax.rem(col + col_offset + n_col, n_col))

    def at_row(offset):
        return at(offset, 0)

    def at_col(offset):
        return at(0, offset)

    depth = n_col // 2
    level = lax.rem(col, depth)
    beside = 2 - 4 * half
    sibling = at_row(1 - 2 * core)
    partner = at_row(beside)
    across = at_row(6 * core - 3)
    turn = at(
        jnp.where(jnp.logical_or(level == 0, level == depth - 1), beside, 0),
        jnp.where(level == depth - 1, 1, jnp.where(level == 0, -1, depth)),
    )

    barrier = pltpu.get_barrier_semaphore()
    peers = (at_row(4), at_row(-4), sibling, partner, across, at_col(1), at_col(-1), turn)
    for peer in peers:
        pl.semaphore_signal(barrier, inc=1, device_id=peer, device_id_type=MESH)

    loads = [pltpu.make_async_copy(ref, raw.at[d], load_sem.at[d]) for d, ref in enumerate((txt_ref, img_ref))]
    for load in loads:
        load.start()
    for load in loads:
        load.wait()

    def normalise(d, c):
        span = pl.ds(c * part, part)
        values = raw[d, span, :].astype(jnp.float32)
        inverse = lax.rsqrt(jnp.sum(values * values, axis=-1, keepdims=True) + eps_norm)
        inv[d, span, :] = inverse
        buf[d, OWN, span, :] = (values * inverse).astype(jnp.bfloat16)

    for c in range(CHUNKS):
        for d in range(2):
            normalise(d, c)

    pl.semaphore_wait(barrier, len(peers))

    def copy(d, number, source, slot, c, target):
        span = pl.ds(c * part, part)
        return pltpu.make_async_remote_copy(
            src_ref=buf.at[d, source, span],
            dst_ref=buf.at[d, slot, span],
            send_sem=send_sem.at[d, number, c],
            recv_sem=recv_sem.at[d, slot, c],
            device_id=target,
            device_id_type=MESH,
        )

    def when(*conditions):
        return pl.when(functools.reduce(jnp.logical_and, conditions))

    places = []
    for d in range(2):
        z = level if d == 0 else depth - 1 - level
        places.append((1 - 2 * d, half if d == 0 else 1 - half, core if d == 0 else 1 - core, z == depth - 1, z == 0))

    def first_sends(d, c):
        sign, h, e, last, _ = places[d]
        copy(d, 3, OWN, 4, c, at_row(4 * sign)).start()

        @when(jnp.logical_not(last), h == 0)
        def _():
            copy(d, 5, OWN, 2, c, partner).start()

        @when(jnp.logical_not(last))
        def _():
            copy(d, 0, OWN, COL + 1, c, at_col(sign)).start()

        @when(e == 0)
        def _():
            copy(d, 6, OWN, 1, c, sibling).start()

    def arrived(d, slot, c):
        copy(d, 0, OWN, slot, c, sibling).wait_recv()

    def pass_on(d, slot, c):
        arrived(d, slot, c)
        sign, h, e, last, _ = places[d]
        if slot == COL + 1 or slot == COL + 2:
            copy(d, slot - COL, slot, slot + 1, c, at_col(sign)).start()
        elif slot == VIA:
            copy(d, 0, VIA, COL + 1, c, turn).start()
            copy(d, 10, VIA, 2, c, at_row(4 * sign)).start()
        elif slot == 4:

            @when(h == 1, jnp.logical_not(last))
            def _():
                copy(d, 5, 4, 2, c, partner).start()

            @when(e == 1)
            def _():
                copy(d, 6, 4, 7, c, across).start()

            copy(d, 8, 4, 5 - 2 * e, c, sibling).start()
        elif slot == 2:

            @when(h == 1, last)
            def _():
                copy(d, 0, 2, COL + 1, c, turn).start()

            copy(d, 4, 2, 6, c, at_row(4 * sign)).start()
            copy(d, 7, 2, 3 - 2 * e, c, sibling).start()
        elif slot == 6:
            copy(d, 9, 6, 7 - 2 * e, c, sibling).start()

    for c in range(CHUNKS):
        for d in range(2):

            @pl.when(places[d][3])
            def _(d=d, c=c):
                copy(d, 5, OWN, jnp.where(places[d][1] == 0, 2, VIA), c, partner).start()

    for c in range(CHUNKS):
        for d in range(2):
            first_sends(d, c)

    scale = jnp.exp(jnp.full((1, rows), scale_ref[0, 0], jnp.float32))
    bias = bias_ref[0, 0]

    def meet(d, slot, on_diagonal=False):
        other = buf[d, slot]
        cosines = lax.dot_general(
            buf[1 - d, OWN], other, (((1,), (1,)), ((), ())), preferred_element_type=jnp.float32
        )
        chance = jax.nn.sigmoid(scale * cosines + bias)
        if on_diagonal:
            across_rows = lax.broadcasted_iota(jnp.int32, (rows, rows), 0)
            across_cols = lax.broadcasted_iota(jnp.int32, (rows, rows), 1)
            chance = chance - jnp.where(across_rows == across_cols, 1.0, 0.0)
        weights = (scale * chance).astype(jnp.bfloat16)
        term = jnp.dot(weights, other, preferred_element_type=jnp.float32)
        acc[d] = term if on_diagonal else acc[d] + term

    def meet_both(slot, on_diagonal=False):
        for d in range(2):
            meet(d, slot, on_diagonal)

    def land(slot):
        for c in range(CHUNKS):
            for d in range(2):
                arrived(d, slot, c)

    def pass_if(condition, d, slot, c):
        @pl.when(condition)
        def _():
            pass_on(d, slot, c)

    wraps = jnp.logical_or(level == 0, level == depth - 1)
    within = jnp.logical_not(wraps)

    def on_last(slot, c, *more):
        for d in range(2):
            pass_if(functools.reduce(jnp.logical_and, [f(d) for f in more], places[d][3]), d, slot, c)

    def on_fresh(slot, c):
        for d in range(2):
            pass_if(places[d][4], d, slot, c)

    def near(d):
        return places[d][1] == 0

    def far(d):
        return places[d][1] == 1

    def inside(slot, c, side=None):
        for d in range(2):
            pass_if(within if side is None else jnp.logical_and(within, side(d)), d, slot, c)

    meet_both(OWN, True)
    for c in range(CHUNKS):
        on_last(VIA, c, near)
        on_last(2, c, far)
        for d in range(2):
            pass_on(d, 4, c)
        inside(COL + 1, c)
        inside(2, c, far)
    meet_both(4)
    for c in range(CHUNKS):
        on_fresh(COL + 1, c)
    for c in range(CHUNKS):
        inside(COL + 2, c)
        inside(2, c, near)
        inside(6, c, far)
        on_last(2, c, near)
        on_fresh(2, c)
        if c == 0:
            on_last(6, 0, far)
    for c in range(CHUNKS):
        on_last(COL + 1, c)
    meet_both(COL + 1)
    land(1)
    meet_both(1)
    meet_both(2)
    for c in range(CHUNKS):
        inside(6, c, near)
        on_last(COL + 2, c)
        if c == 0:
            land(3)
            meet_both(3)
    on_last(6, 1, far)
    for c in range(CHUNKS):
        on_last(6, c, near)
        on_fresh(6, c)
        on_fresh(COL + 2, c)
    meet_both(6)
    land(5)
    meet_both(5)
    land(7)
    meet_both(7)
    meet_both(COL + 2)
    land(COL + 3)
    meet_both(COL + 3)

    for d, out in ((0, img_out), (1, txt_out)):
        inverse = inv[1 - d]
        unit = raw[1 - d].astype(jnp.float32) * inverse
        direction = acc[d]
        along = jnp.sum(unit * direction, axis=-1, keepdims=True)
        out[...] = inverse * (direction - unit * along)

    for d in range(2):
        for number in range(10):
            for c in range(CHUNKS):
                copy(d, number, OWN, 1, c, sibling).wait_send()
        for c in range(CHUNKS):

            @when(places[d][3], places[d][1] == 0)
            def _(d=d, c=c):
                copy(d, 10, OWN, 1, c, sibling).wait_send()


def on_device(n_row, n_col, picture, caption, scale_exponent, offset):
    rows, width = picture.shape
    scalar = pl.BlockSpec(memory_space=pltpu.SMEM)
    whole = pl.BlockSpec(memory_space=pltpu.HBM)
    out = jax.ShapeDtypeStruct((rows, width), jnp.float32)
    return pl.pallas_call(
        functools.partial(kernel, n_row, n_col),
        out_shape=(out, out),
        in_specs=[scalar, scalar, whole, whole],
        out_specs=[pl.BlockSpec(memory_space=pltpu.VMEM)] * 2,
        scratch_shapes=[
            pltpu.VMEM((2, rows, width), jnp.bfloat16),
            pltpu.VMEM((2, 12, rows, width), jnp.bfloat16),
            pltpu.VMEM((2, rows, width), jnp.float32),
            pltpu.VMEM((2, rows, 1), jnp.float32),
            pltpu.SemaphoreType.DMA((2, 11, CHUNKS)),
            pltpu.SemaphoreType.DMA((2, 12, CHUNKS)),
            pltpu.SemaphoreType.DMA((2,)),
        ],
        compiler_params=pltpu.CompilerParams(
            collective_id=0, has_side_effects=True, vmem_limit_bytes=48 << 20
        ),
    )(
        scale_exponent.reshape(1, 1),
        offset.reshape(1, 1),
        pltpu.with_memory_space_constraint(caption, pltpu.HBM),
        pltpu.with_memory_space_constraint(picture, pltpu.HBM),
    )


def solution(mesh):
    return jax.shard_map(
        functools.partial(on_device, mesh.shape["row"], mesh.shape["col"]),
        mesh=mesh,
        in_specs=(P(("row", "col"), None), P(("row", "col"), None), P(), P()),
        out_specs=(P(("row", "col"), None), P(("row", "col"), None)),
        check_vma=False,
    )
```

```python
import functools

import jax
import jax.numpy as jnp
from jax import lax
from jax.experimental import pallas as pl
from jax.experimental.pallas import tpu as pltpu
from jax.sharding import PartitionSpec as P

MESH = pl.DeviceIdType.MESH
eps_norm = 1e-06

OWN, COL, VIA = 0, 7, 11
CHUNKS = 2
TEXT, IMAGE = 0, 1
NEAR, FAR = 0, 1


def kernel(
    n_row, n_col, scale_ref, bias_ref, txt_ref, img_ref, img_out, txt_out, raw, buf, acc, inv, send_sem, recv_sem, load_sem, open_sem
):
    rows, width = txt_ref.shape
    part = rows // CHUNKS
    row, col = lax.axis_index("row"), lax.axis_index("col")
    core = lax.rem(row, 2)
    half = lax.rem(row // 2, 2)
    depth = n_col // 2
    level = lax.rem(col, depth)
    top, bottom = level == depth - 1, level == 0

    def at(row_offset, col_offset):
        return (lax.rem(row + row_offset + n_row, n_row), lax.rem(col + col_offset + n_col, n_col))

    def at_row(offset):
        return at(offset, 0)

    def at_col(offset):
        return at(0, offset)

    beside = 2 - 4 * half
    sibling = at_row(1 - 2 * core)
    partner = at_row(beside)
    across = at_row(6 * core - 3)
    turn = at(beside, jnp.where(top, 1, -1))
    crossing = at_col(depth)
    before = level == depth - 2

    barrier = pltpu.get_barrier_semaphore()

    def greet(peer):
        pl.semaphore_signal(barrier, inc=1, device_id=peer, device_id_type=MESH)

    for peer in (at_row(4), at_row(-4), sibling, partner, across, at_col(-1)):
        greet(peer)

    @pl.when(jnp.logical_not(top))
    def _():
        greet(at_col(1))

    @pl.when(bottom)
    def _():
        greet(turn)
        greet(at_col(depth - 2))

    @pl.when(before)
    def _():
        greet(crossing)

    loads = [pltpu.make_async_copy(ref, raw.at[d], load_sem.at[d]) for d, ref in enumerate((txt_ref, img_ref))]
    for load in loads:
        load.start()
    for load in loads:
        load.wait()

    def normalise(d, c):
        span = pl.ds(c * part, part)
        values = raw[d, span, :].astype(jnp.float32)
        inverse = lax.rsqrt(jnp.sum(values * values, axis=-1, keepdims=True) + eps_norm)
        inv[d, span, :] = inverse
        buf[d, OWN, span, :] = (values * inverse).astype(jnp.bfloat16)

    for c in range(CHUNKS):
        for d in range(2):
            normalise(d, c)

    pl.semaphore_wait(barrier, 7 + jnp.where(top, 1, 0) + jnp.where(before, 2, 0) - jnp.where(bottom, 1, 0))

    @pl.when(top)
    def _():
        for peer in (at_col(1), turn):
            pl.semaphore_signal(open_sem, inc=1, device_id=peer, device_id_type=MESH)

    def copy(d, number, source, slot, c, target):
        span = pl.ds(c * part, part)
        return pltpu.make_async_remote_copy(
            src_ref=buf.at[d, source, span],
            dst_ref=buf.at[d, slot, span],
            send_sem=send_sem.at[d, number, c],
            recv_sem=recv_sem.at[d, slot, c],
            device_id=target,
            device_id_type=MESH,
        )

    def when(*conditions):
        return pl.when(functools.reduce(jnp.logical_and, conditions))

    signs = (1, -1)
    sides = (half, 1 - half)
    ends = (core, 1 - core)
    lasts = (top, bottom)

    def first_sends(d, c):
        copy(d, 3, OWN, 4, c, at_row(4 * signs[d])).start()

        @when(jnp.logical_not(lasts[d]), sides[d] == 0)
        def _():
            copy(d, 5, OWN, 2, c, partner).start()

        @when(jnp.logical_not(lasts[d]))
        def _():
            copy(d, 0, OWN, COL + 1, c, at_col(signs[d])).start()

        if d == TEXT:

            @pl.when(before)
            def _():
                copy(d, 10, OWN, VIA, c, crossing).start()

        @when(ends[d] == 0)
        def _():
            copy(d, 6, OWN, 1, c, sibling).start()

    def arrived(d, slot, c):
        copy(d, 0, OWN, slot, c, sibling).wait_recv()

    def pass_on(d, slot, c):
        arrived(d, slot, c)
        sign, h, e, last = signs[d], sides[d], ends[d], lasts[d]
        if slot == COL + 1:
            if d == TEXT:

                @pl.when(jnp.logical_not(last))
                def _():
                    copy(d, 1, slot, slot + 1, c, at_col(sign)).start()

            else:
                copy(d, 1, slot, slot + 1, c, at_col(sign)).start()
        elif slot == COL + 2:
            copy(d, 2, slot, slot + 1, c, at_col(sign)).start()
        elif slot == VIA:
            if d == TEXT:
                copy(d, 0, VIA, COL + 1, c, turn).start()
            copy(d, 10, VIA, 2, c, at_row(4 * sign)).start()
        elif slot == 4:

            @when(h == 1, jnp.logical_not(last))
            def _():
                copy(d, 5, 4, 2, c, partner).start()

            @when(e == 1)
            def _():
                copy(d, 6, 4, 7, c, across).start()

            copy(d, 8, 4, 5 - 2 * e, c, sibling).start()
        elif slot == 2:
            if d == TEXT:

                @when(h == 1, last)
                def _():
                    copy(d, 0, 2, COL + 1, c, turn).start()

            copy(d, 4, 2, 6, c, at_row(4 * sign)).start()
            copy(d, 7, 2, 3 - 2 * e, c, sibling).start()
        elif slot == 6:
            copy(d, 9, 6, 7 - 2 * e, c, sibling).start()

    for c in range(CHUNKS):
        for d in range(2):

            @pl.when(lasts[d])
            def _(d=d, c=c):
                copy(d, 5, OWN, jnp.where(sides[d] == 0, 2, VIA), c, partner).start()

    for c in range(CHUNKS):
        for d in range(2):
            first_sends(d, c)

    scale = jnp.exp(jnp.full((1, rows), scale_ref[0, 0], jnp.float32))
    bias = bias_ref[0, 0]

    def meet(slot, on_diagonal=False):
        for d in range(2):
            other = buf[d, slot]
            cosines = lax.dot_general(
                buf[1 - d, OWN], other, (((1,), (1,)), ((), ())), preferred_element_type=jnp.float32
            )
            chance = jax.nn.sigmoid(scale * cosines + bias)
            if on_diagonal:
                across_rows = lax.broadcasted_iota(jnp.int32, (rows, rows), 0)
                across_cols = lax.broadcasted_iota(jnp.int32, (rows, rows), 1)
                chance = chance - jnp.where(across_rows == across_cols, 1.0, 0.0)
            weights = (scale * chance).astype(jnp.bfloat16)
            term = jnp.dot(weights, other, preferred_element_type=jnp.float32)
            acc[d] = term if on_diagonal else acc[d] + term

    def land(slot):
        for c in range(CHUNKS):
            for d in range(2):
                arrived(d, slot, c)

    def step(last, what, *more):
        if what == "open":
            pl.semaphore_wait(open_sem, 2)
        elif what == "turn":
            (c,) = more
            copy(last, 0, jnp.where(sides[last] == 0, VIA, 2), COL + 1, c, turn).start()
        elif what == "handed":
            (c,) = more
            pl.when(sides[last] == 0)(lambda: pass_on(last, VIA, c))
            pl.when(sides[last] == 1)(lambda: pass_on(last, 2, c))
        elif what == "both":
            slot, c = more
            pass_on(0, slot, c)
            pass_on(1, slot, c)
        else:
            slot, side, c = more
            d = last if what == "last" else 1 - last
            if side is None:
                pass_on(d, slot, c)
            else:
                pl.when(sides[d] == side)(lambda: pass_on(d, slot, c))

    def at_wrap(here, last, items):
        @pl.when(here)
        def _():
            for item in items:
                step(last, *item)

    def within(items):
        @when(jnp.logical_not(top), jnp.logical_not(bottom))
        def _():
            for slot, side, c in items:
                for d in range(2):
                    if side is None:
                        pass_on(d, slot, c)
                    else:
                        pl.when(sides[d] == side)(functools.partial(pass_on, d, slot, c))
                if slot == 2 and side == 1:

                    @pl.when(before)
                    def _(c=c):
                        arrived(TEXT, VIA, c)
                        copy(TEXT, 11, VIA, COL + 2, c, at_col(2 - depth)).start()

    meet(OWN, True)
    within([(slot, side, c) for c in range(CHUNKS) for slot, side in ((4, None), (COL + 1, None), (2, 1))])
    at_wrap(bottom, IMAGE, (
            ("handed", 0),
            ("both", 4, 0),
            ("open",),
            ("turn", 0),
            ("handed", 1),
            ("turn", 1),
            ("both", 4, 1),
        ))
    at_wrap(top, TEXT, (
            ("handed", 0),
            ("both", 4, 0),
            ("handed", 1),
            ("both", 4, 1),
        ))
    meet(4)
    within([(slot, side, c) for c in range(CHUNKS) for slot, side in ((COL + 2, None), (2, 0), (6, 1))])
    at_wrap(bottom, IMAGE, (
            ("last", 2, NEAR, 0),
            ("fresh", 2, None, 0),
            ("last", 6, FAR, 0),
            ("last", 2, NEAR, 1),
            ("fresh", 2, None, 1),
            ("last", 6, FAR, 1),
            ("fresh", COL + 1, None, 0),
            ("fresh", COL + 1, None, 1),
        ))
    at_wrap(top, TEXT, (
            ("fresh", COL + 1, None, 0),
            ("fresh", COL + 1, None, 1),
            ("last", 2, NEAR, 0),
            ("fresh", 2, None, 0),
            ("last", COL + 2, None, 0),
            ("last", 6, FAR, 0),
            ("last", 2, NEAR, 1),
            ("fresh", 2, None, 1),
            ("last", COL + 2, None, 1),
            ("last", 6, FAR, 1),
            ("last", COL + 1, None, 0),
            ("last", COL + 1, None, 1),
        ))
    meet(2)
    within([(6, 0, c) for c in range(CHUNKS)])
    at_wrap(bottom, IMAGE, (
            ("fresh", 6, None, 0),
            ("fresh", 6, None, 1),
            ("last", 6, NEAR, 0),
            ("fresh", COL + 2, None, 0),
            ("last", COL + 1, None, 0),
            ("last", COL + 1, None, 1),
            ("fresh", COL + 2, None, 1),
            ("last", 6, NEAR, 1),
            ("last", COL + 2, None, 0),
            ("last", COL + 2, None, 1),
        ))
    at_wrap(top, TEXT, (
            ("fresh", 6, None, 0),
            ("fresh", COL + 2, None, 0),
            ("last", 6, NEAR, 0),
            ("fresh", 6, None, 1),
            ("fresh", COL + 2, None, 1),
            ("last", 6, NEAR, 1),
        ))
    meet(COL + 1)
    meet(6)
    for slot in (1, 3, 5, 7):
        land(slot)
        meet(slot)
    meet(COL + 2)
    land(COL + 3)
    meet(COL + 3)

    for d, out in ((0, img_out), (1, txt_out)):
        inverse = inv[1 - d]
        unit = raw[1 - d].astype(jnp.float32) * inverse
        direction = acc[d]
        along = jnp.sum(unit * direction, axis=-1, keepdims=True)
        out[...] = inverse * (direction - unit * along)

    for d in range(2):
        for number in range(12):
            for c in range(CHUNKS):

                def sent(d=d, number=number, c=c):
                    copy(d, number, OWN, 1, c, sibling).wait_send()

                handed = jnp.logical_and(lasts[d], sides[d] == 0)
                if number == 1 and d == TEXT:
                    pl.when(jnp.logical_not(top))(sent)
                elif number == 10:
                    pl.when(jnp.logical_or(handed, before) if d == TEXT else handed)(sent)
                elif number == 11:
                    if d == TEXT:
                        pl.when(before)(sent)
                else:
                    sent()


def on_device(n_row, n_col, picture, caption, scale_exponent, offset):
    rows, width = picture.shape
    scalar = pl.BlockSpec(memory_space=pltpu.SMEM)
    whole = pl.BlockSpec(memory_space=pltpu.HBM)
    out = jax.ShapeDtypeStruct((rows, width), jnp.float32)
    return pl.pallas_call(
        functools.partial(kernel, n_row, n_col),
        out_shape=(out, out),
        in_specs=[scalar, scalar, whole, whole],
        out_specs=[pl.BlockSpec(memory_space=pltpu.VMEM)] * 2,
        scratch_shapes=[
            pltpu.VMEM((2, rows, width), jnp.bfloat16),
            pltpu.VMEM((2, 12, rows, width), jnp.bfloat16),
            pltpu.VMEM((2, rows, width), jnp.float32),
            pltpu.VMEM((2, rows, 1), jnp.float32),
            pltpu.SemaphoreType.DMA((2, 12, CHUNKS)),
            pltpu.SemaphoreType.DMA((2, 12, CHUNKS)),
            pltpu.SemaphoreType.DMA((2,)),
            pltpu.SemaphoreType.REGULAR,
        ],
        compiler_params=pltpu.CompilerParams(
            collective_id=0, has_side_effects=True, vmem_limit_bytes=48 << 20
        ),
    )(
        scale_exponent.reshape(1, 1),
        offset.reshape(1, 1),
        pltpu.with_memory_space_constraint(caption, pltpu.HBM),
        pltpu.with_memory_space_constraint(picture, pltpu.HBM),
    )


def solution(mesh):
    return jax.shard_map(
        functools.partial(on_device, mesh.shape["row"], mesh.shape["col"]),
        mesh=mesh,
        in_specs=(P(("row", "col"), None), P(("row", "col"), None), P(), P()),
        out_specs=(P(("row", "col"), None), P(("row", "col"), None)),
        check_vma=False,
    )
```

```python
import functools

import jax
import jax.numpy as jnp
from jax import lax
from jax.experimental import pallas as pl
from jax.experimental.pallas import tpu as pltpu
from jax.sharding import PartitionSpec as P

MESH = pl.DeviceIdType.MESH
eps_norm = 1e-06

OWN, COL, VIA = 0, 7, 11
CHUNKS = 4
TEXT, IMAGE = 0, 1
NEAR, FAR = 0, 1


def kernel(
    n_row, n_col, scale_ref, bias_ref, txt_ref, img_ref, img_out, txt_out, raw, buf, acc, inv, send_sem, recv_sem, load_sem, open_sem
):
    rows, width = txt_ref.shape
    part = rows // CHUNKS
    row, col = lax.axis_index("row"), lax.axis_index("col")
    core = lax.rem(row, 2)
    half = lax.rem(row // 2, 2)
    depth = n_col // 2
    level = lax.rem(col, depth)
    top, bottom = level == depth - 1, level == 0

    def at(row_offset, col_offset):
        return (lax.rem(row + row_offset + n_row, n_row), lax.rem(col + col_offset + n_col, n_col))

    def at_row(offset):
        return at(offset, 0)

    def at_col(offset):
        return at(0, offset)

    beside = 2 - 4 * half
    sibling = at_row(1 - 2 * core)
    partner = at_row(beside)
    across = at_row(6 * core - 3)
    turn = at(beside, jnp.where(top, 1, -1))
    crossing = at_col(depth)
    befores = (level == depth - 2, level == 1)

    barrier = pltpu.get_barrier_semaphore()

    def greet(peer):
        pl.semaphore_signal(barrier, inc=1, device_id=peer, device_id_type=MESH)

    for peer in (at_row(4), at_row(-4), sibling, partner, across, at_col(-1)):
        greet(peer)

    @pl.when(jnp.logical_not(top))
    def _():
        greet(at_col(1))

    @pl.when(bottom)
    def _():
        greet(turn)

    @pl.when(level < 2)
    def _():
        greet(at_col(depth - 2))

    @pl.when(jnp.logical_or(*befores))
    def _():
        greet(crossing)

    def load(d, c):
        span = pl.ds(c * part, part)
        return pltpu.make_async_copy((txt_ref, img_ref)[d].at[span], raw.at[d, span], load_sem.at[d, c])

    for d in range(2):
        for c in range(CHUNKS):
            load(d, c).start()

    def normalise(d, c):
        load(d, c).wait()
        span = pl.ds(c * part, part)
        values = raw[d, span, :].astype(jnp.float32)
        inverse = lax.rsqrt(jnp.sum(values * values, axis=-1, keepdims=True) + eps_norm)
        inv[d, span, :] = inverse
        buf[d, OWN, span, :] = (values * inverse).astype(jnp.bfloat16)

    for c in range(CHUNKS):
        normalise(TEXT, c)

    pl.semaphore_wait(barrier, 7 + jnp.where(level >= depth - 2, 2, 0) + jnp.where(level == 1, 1, 0) - jnp.where(bottom, 1, 0))

    @pl.when(top)
    def _():
        for peer in (at_col(1), turn, at_col(2 - depth)):
            pl.semaphore_signal(open_sem, inc=1, device_id=peer, device_id_type=MESH)

    def copy(d, number, source, slot, c, target):
        span = pl.ds(c * part, part)
        return pltpu.make_async_remote_copy(
            src_ref=buf.at[d, source, span],
            dst_ref=buf.at[d, slot, span],
            send_sem=send_sem.at[d, number, c],
            recv_sem=recv_sem.at[d, slot, c],
            device_id=target,
            device_id_type=MESH,
        )

    def when(*conditions):
        return pl.when(functools.reduce(jnp.logical_and, conditions))

    signs = (1, -1)
    sides = (half, 1 - half)
    ends = (core, 1 - core)
    lasts = (top, bottom)

    def first_sends(d, c):
        copy(d, 3, OWN, 4, c, at_row(4 * signs[d])).start()

        @when(jnp.logical_not(lasts[d]), sides[d] == 0)
        def _():
            copy(d, 5, OWN, 2, c, partner).start()

        @when(jnp.logical_not(lasts[d]))
        def _():
            copy(d, 0, OWN, COL + 1, c, at_col(signs[d])).start()

        @pl.when(befores[d])
        def _():
            copy(d, 10, OWN, VIA, c, crossing).start()

        @when(ends[d] == 0)
        def _():
            copy(d, 6, OWN, 1, c, sibling).start()

    def arrived(d, slot, c):
        copy(d, 0, OWN, slot, c, sibling).wait_recv()

    def forward(d, slot, c):
        sign, h, e, last = signs[d], sides[d], ends[d], lasts[d]
        if slot == COL + 1:

            @pl.when(jnp.logical_not(last))
            def _():
                copy(d, 1, slot, slot + 1, c, at_col(sign)).start()

        elif slot == COL + 2:
            copy(d, 2, slot, slot + 1, c, at_col(sign)).start()
        elif slot == VIA:
            if d == TEXT:
                copy(d, 0, VIA, COL + 1, c, turn).start()
            copy(d, 10, VIA, 2, c, at_row(4 * sign)).start()
        elif slot == 4:

            @when(h == 1, jnp.logical_not(last))
            def _():
                copy(d, 5, 4, 2, c, partner).start()

            @when(e == 1)
            def _():
                copy(d, 6, 4, 7, c, across).start()

            copy(d, 8, 4, 5 - 2 * e, c, sibling).start()
        elif slot == 2:
            if d == TEXT:

                @when(h == 1, last)
                def _():
                    copy(d, 0, 2, COL + 1, c, turn).start()

            copy(d, 4, 2, 6, c, at_row(4 * sign)).start()
            copy(d, 7, 2, 3 - 2 * e, c, sibling).start()
        elif slot == 6:
            copy(d, 9, 6, 7 - 2 * e, c, sibling).start()

    def hand_over(d):
        @pl.when(lasts[d])
        def _():
            for c in range(CHUNKS):
                copy(d, 5, OWN, jnp.where(sides[d] == 0, 2, VIA), c, partner).start()

    hand_over(TEXT)
    for c in range(CHUNKS):
        normalise(IMAGE, c)
    hand_over(IMAGE)
    for c in range(CHUNKS):
        for d in range(2):
            first_sends(d, c)

    scale = jnp.exp(jnp.full((1, rows), scale_ref[0, 0], jnp.float32))
    bias = bias_ref[0, 0]

    def meet(slot, directions=(TEXT, IMAGE), on_diagonal=False):
        for d in directions:
            other = buf[d, slot]
            cosines = lax.dot_general(
                buf[1 - d, OWN], other, (((1,), (1,)), ((), ())), preferred_element_type=jnp.float32
            )
            chance = jax.nn.sigmoid(scale * cosines + bias)
            if on_diagonal:
                across_rows = lax.broadcasted_iota(jnp.int32, (rows, rows), 0)
                across_cols = lax.broadcasted_iota(jnp.int32, (rows, rows), 1)
                chance = chance - jnp.where(across_rows == across_cols, 1.0, 0.0)
            weights = (scale * chance).astype(jnp.bfloat16)
            term = jnp.dot(weights, other, preferred_element_type=jnp.float32)
            acc[d] = term if on_diagonal else acc[d] + term

    pieces = (range(CHUNKS // 2), range(CHUNKS // 2, CHUNKS))

    def see(d, slot):
        for c in range(CHUNKS):
            arrived(d, slot, c)

    def land(slot):
        see(TEXT, slot)
        see(IMAGE, slot)

    def pass_on(d, slot, piece, side=None, wait=True):
        def run():
            for c in pieces[piece]:
                if wait:
                    arrived(d, slot, c)
                forward(d, slot, c)

        if side is None:
            run()
        else:
            pl.when(sides[d] == side)(run)

    def pass_both(slot, piece, side=None):
        pass_on(TEXT, slot, piece, side)
        pass_on(IMAGE, slot, piece, side)

    def handed(d, piece):
        pass_on(d, VIA, piece, NEAR)
        pass_on(d, 2, piece, FAR)

    def cross(d, piece):
        if d == IMAGE and piece == 0:
            pl.semaphore_wait(open_sem, 1)
        for c in pieces[piece]:
            arrived(d, VIA, c)
            copy(d, 11, VIA, COL + 2, c, at_col(signs[d] * (2 - depth))).start()

    def turn_back(piece):
        for c in pieces[piece]:
            copy(IMAGE, 0, jnp.where(sides[IMAGE] == 0, VIA, 2), COL + 1, c, turn).start()

    def finish(d):
        see(d, COL + 3)
        meet(COL + 3, (d,))
        inverse = inv[1 - d]
        unit = raw[1 - d].astype(jnp.float32) * inverse
        direction = acc[d]
        along = jnp.sum(unit * direction, axis=-1, keepdims=True)
        (img_out, txt_out)[d][...] = inverse * (direction - unit * along)

    meet(OWN, on_diagonal=True)

    @when(jnp.logical_not(top), jnp.logical_not(bottom))
    def _():
        for piece in range(2):
            pass_both(4, piece)
            pass_both(COL + 1, piece)
            pass_both(2, piece, FAR)
            for d in range(2):
                pl.when(befores[d])(functools.partial(cross, d, piece))
        meet(4)
        meet(COL + 1)
        for piece in range(2):
            pass_both(COL + 2, piece)
            pass_both(2, piece, NEAR)
            pass_both(6, piece, FAR)
        meet(COL + 2)
        meet(2)
        land(3)
        meet(3)
        pass_both(6, 0, NEAR)
        land(1)
        meet(1)
        pass_both(6, 1, NEAR)
        meet(6)
        for slot in (5, 7):
            land(slot)
            meet(slot)
        finish(TEXT)
        finish(IMAGE)

    @pl.when(bottom)
    def _():
        handed(IMAGE, 0)
        pass_both(4, 0)
        pl.semaphore_wait(open_sem, 2)
        turn_back(0)
        handed(IMAGE, 1)
        turn_back(1)
        pass_both(4, 1)
        meet(4)
        see(IMAGE, COL + 1)
        meet(COL + 1, (IMAGE,))
        pass_on(IMAGE, 2, 0, NEAR)
        pass_on(TEXT, 2, 0)
        pass_on(IMAGE, 6, 0, FAR)
        pass_on(TEXT, COL + 1, 0)
        pass_on(IMAGE, 2, 1, NEAR)
        pass_on(TEXT, 2, 1)
        pass_on(IMAGE, 6, 1, FAR)
        pass_on(TEXT, COL + 1, 1)
        meet(2)
        pass_on(TEXT, 6, 0)
        meet(COL + 1, (TEXT,))
        pass_on(TEXT, 6, 1)
        meet(6, (TEXT,))
        pass_on(IMAGE, COL + 2, 0)
        pass_on(IMAGE, COL + 2, 1)
        pass_on(IMAGE, 6, 0, NEAR)
        pass_on(TEXT, COL + 2, 0)
        land(3)
        meet(3)
        meet(COL + 2, (IMAGE,))
        pass_on(IMAGE, 6, 1, NEAR)
        land(1)
        meet(1)
        pass_on(TEXT, COL + 2, 1)
        meet(6, (IMAGE,))
        meet(COL + 2, (TEXT,))
        for slot in (5, 7):
            land(slot)
            meet(slot)
        finish(IMAGE)
        finish(TEXT)

    @pl.when(top)
    def _():
        for piece in range(2):
            handed(TEXT, piece)
            pass_both(4, piece)
        meet(4)
        see(TEXT, COL + 1)
        meet(COL + 1, (TEXT,))
        pass_on(IMAGE, COL + 1, 0)
        pass_on(IMAGE, COL + 1, 1)
        for piece in range(2):
            pass_on(TEXT, 2, piece, NEAR)
            pass_on(IMAGE, 2, piece)
            pass_on(TEXT, COL + 2, piece)
            pass_on(TEXT, 6, piece, FAR)
        meet(COL + 1, (IMAGE,))
        meet(2)
        meet(COL + 2, (TEXT,))
        pass_on(IMAGE, 6, 0)
        pass_on(IMAGE, COL + 2, 0)
        land(3)
        meet(3)
        pass_on(TEXT, 6, 0, NEAR)
        pass_on(IMAGE, 6, 1)
        pass_on(IMAGE, COL + 2, 1)
        land(1)
        meet(1)
        pass_on(TEXT, 6, 1, NEAR)
        meet(6)
        meet(COL + 2, (IMAGE,))
        for slot in (5, 7):
            land(slot)
            meet(slot)
        finish(TEXT)
        finish(IMAGE)

    for d in range(2):
        for number in range(12):
            for c in range(CHUNKS):

                def sent(d=d, number=number, c=c):
                    copy(d, number, OWN, 1, c, sibling).wait_send()

                handed = jnp.logical_and(lasts[d], sides[d] == 0)
                if number == 1:
                    pl.when(jnp.logical_not(lasts[d]))(sent)
                elif number == 10:
                    pl.when(jnp.logical_or(handed, befores[d]))(sent)
                elif number == 11:
                    pl.when(befores[d])(sent)
                else:
                    sent()


def on_device(n_row, n_col, picture, caption, scale_exponent, offset):
    rows, width = picture.shape
    scalar = pl.BlockSpec(memory_space=pltpu.SMEM)
    whole = pl.BlockSpec(memory_space=pltpu.HBM)
    out = jax.ShapeDtypeStruct((rows, width), jnp.float32)
    return pl.pallas_call(
        functools.partial(kernel, n_row, n_col),
        out_shape=(out, out),
        in_specs=[scalar, scalar, whole, whole],
        out_specs=[pl.BlockSpec(memory_space=pltpu.VMEM)] * 2,
        scratch_shapes=[
            pltpu.VMEM((2, rows, width), jnp.bfloat16),
            pltpu.VMEM((2, 12, rows, width), jnp.bfloat16),
            pltpu.VMEM((2, rows, width), jnp.float32),
            pltpu.VMEM((2, rows, 1), jnp.float32),
            pltpu.SemaphoreType.DMA((2, 12, CHUNKS)),
            pltpu.SemaphoreType.DMA((2, 12, CHUNKS)),
            pltpu.SemaphoreType.DMA((2, CHUNKS)),
            pltpu.SemaphoreType.REGULAR,
        ],
        compiler_params=pltpu.CompilerParams(
            collective_id=0, has_side_effects=True, vmem_limit_bytes=48 << 20
        ),
    )(
        scale_exponent.reshape(1, 1),
        offset.reshape(1, 1),
        pltpu.with_memory_space_constraint(caption, pltpu.HBM),
        pltpu.with_memory_space_constraint(picture, pltpu.HBM),
    )


def solution(mesh):
    return jax.shard_map(
        functools.partial(on_device, mesh.shape["row"], mesh.shape["col"]),
        mesh=mesh,
        in_specs=(P(("row", "col"), None), P(("row", "col"), None), P(), P()),
        out_specs=(P(("row", "col"), None), P(("row", "col"), None)),
        check_vma=False,
    )
```

```python
import functools

import jax
import jax.numpy as jnp
from jax import lax
from jax.experimental import pallas as pl
from jax.experimental.pallas import tpu as pltpu
from jax.sharding import PartitionSpec as P

MESH = pl.DeviceIdType.MESH
eps_norm = 1e-06

OWN, COL, VIA = 0, 7, 11
CHUNKS = 4
TEXT, IMAGE = 0, 1
NEAR, FAR = 0, 1


def kernel(
    n_row, n_col, scale_ref, bias_ref, txt_ref, img_ref, img_out, txt_out, raw, buf, acc, inv, send_sem, recv_sem, load_sem, open_sem
):
    rows, width = txt_ref.shape
    part = rows // CHUNKS
    row, col = lax.axis_index("row"), lax.axis_index("col")
    core = lax.rem(row, 2)
    half = lax.rem(row // 2, 2)
    depth = n_col // 2
    level = lax.rem(col, depth)
    top, bottom = level == depth - 1, level == 0

    def at(row_offset, col_offset):
        return (lax.rem(row + row_offset + n_row, n_row), lax.rem(col + col_offset + n_col, n_col))

    def at_row(offset):
        return at(offset, 0)

    def at_col(offset):
        return at(0, offset)

    beside = 2 - 4 * half
    sibling = at_row(1 - 2 * core)
    partner = at_row(beside)
    across = at_row(6 * core - 3)
    turn = at(beside, jnp.where(top, 1, -1))
    crossing = at_col(depth)
    befores = (level == depth - 2, level == 1)

    barrier = pltpu.get_barrier_semaphore()

    def greet(peer):
        pl.semaphore_signal(barrier, inc=1, device_id=peer, device_id_type=MESH)

    for peer in (at_row(4), at_row(-4), sibling, partner, across, at_col(-1)):
        greet(peer)

    @pl.when(jnp.logical_not(top))
    def _():
        greet(at_col(1))

    @pl.when(bottom)
    def _():
        greet(turn)

    @pl.when(level < 2)
    def _():
        greet(at_col(depth - 2))

    @pl.when(jnp.logical_or(*befores))
    def _():
        greet(crossing)

    def load(d, c):
        span = pl.ds(c * part, part)
        return pltpu.make_async_copy((txt_ref, img_ref)[d].at[span], raw.at[d, span], load_sem.at[d, c])

    for d in range(2):
        for c in range(CHUNKS):
            load(d, c).start()

    def normalise(d, c):
        load(d, c).wait()
        span = pl.ds(c * part, part)
        values = raw[d, span, :].astype(jnp.float32)
        inverse = lax.rsqrt(jnp.sum(values * values, axis=-1, keepdims=True) + eps_norm)
        inv[d, span, :] = inverse
        buf[d, OWN, span, :] = (values * inverse).astype(jnp.bfloat16)

    for c in range(CHUNKS):
        normalise(TEXT, c)

    pl.semaphore_wait(barrier, 7 + jnp.where(level >= depth - 2, 2, 0) + jnp.where(level == 1, 1, 0) - jnp.where(bottom, 1, 0))

    @pl.when(top)
    def _():
        for peer in (at_col(1), turn, at_col(2 - depth)):
            pl.semaphore_signal(open_sem, inc=1, device_id=peer, device_id_type=MESH)

    def copy(d, number, source, slot, c, target):
        span = pl.ds(c * part, part)
        return pltpu.make_async_remote_copy(
            src_ref=buf.at[d, source, span],
            dst_ref=buf.at[d, slot, span],
            send_sem=send_sem.at[d, number, c],
            recv_sem=recv_sem.at[d, slot, c],
            device_id=target,
            device_id_type=MESH,
        )

    def when(*conditions):
        return pl.when(functools.reduce(jnp.logical_and, conditions))

    signs = (1, -1)
    sides = (half, 1 - half)
    ends = (core, 1 - core)
    lasts = (top, bottom)

    def first_sends(d, c):
        copy(d, 3, OWN, 4, c, at_row(4 * signs[d])).start()

        @when(jnp.logical_not(lasts[d]), sides[d] == 0)
        def _():
            copy(d, 5, OWN, 2, c, partner).start()

        @when(jnp.logical_not(lasts[d]))
        def _():
            copy(d, 0, OWN, COL + 1, c, at_col(signs[d])).start()

        if d == IMAGE:

            @pl.when(befores[d])
            def _():
                copy(d, 10, OWN, VIA, c, crossing).start()

        @when(ends[d] == 0)
        def _():
            copy(d, 6, OWN, 1, c, sibling).start()

    def arrived(d, slot, c):
        copy(d, 0, OWN, slot, c, sibling).wait_recv()

    def forward(d, slot, c):
        sign, h, e, last = signs[d], sides[d], ends[d], lasts[d]
        if slot == COL + 1:

            @pl.when(jnp.logical_not(last))
            def _():
                copy(d, 1, slot, slot + 1, c, at_col(sign)).start()

        elif slot == COL + 2:
            copy(d, 2, slot, slot + 1, c, at_col(sign)).start()
        elif slot == VIA:
            if d == TEXT:
                copy(d, 0, VIA, COL + 1, c, turn).start()
            copy(d, 10, VIA, 2, c, at_row(4 * sign)).start()
        elif slot == 4:

            @when(h == 1, jnp.logical_not(last))
            def _():
                copy(d, 5, 4, 2, c, partner).start()

            @when(e == 1)
            def _():
                copy(d, 6, 4, 7, c, across).start()

            copy(d, 8, 4, 5 - 2 * e, c, sibling).start()
        elif slot == 2:
            if d == TEXT:

                @when(h == 1, last)
                def _():
                    copy(d, 0, 2, COL + 1, c, turn).start()

            copy(d, 4, 2, 6, c, at_row(4 * sign)).start()
            copy(d, 7, 2, 3 - 2 * e, c, sibling).start()
        elif slot == 6:
            copy(d, 9, 6, 7 - 2 * e, c, sibling).start()

    def hand_over(d):
        @pl.when(lasts[d])
        def _():
            for c in range(CHUNKS):
                copy(d, 5, OWN, jnp.where(sides[d] == 0, 2, VIA), c, partner).start()

    hand_over(TEXT)

    @pl.when(befores[TEXT])
    def _():
        for c in range(CHUNKS):
            copy(TEXT, 10, OWN, VIA, c, crossing).start()

    for c in range(CHUNKS):
        normalise(IMAGE, c)
    hand_over(IMAGE)
    for c in range(CHUNKS):
        for d in range(2):
            first_sends(d, c)

    scale = jnp.exp(jnp.full((1, rows), scale_ref[0, 0], jnp.float32))
    bias = bias_ref[0, 0]

    def meet(slot, directions=(TEXT, IMAGE), on_diagonal=False):
        for d in directions:
            other = buf[d, slot]
            cosines = lax.dot_general(
                buf[1 - d, OWN], other, (((1,), (1,)), ((), ())), preferred_element_type=jnp.float32
            )
            chance = jax.nn.sigmoid(scale * cosines + bias)
            if on_diagonal:
                across_rows = lax.broadcasted_iota(jnp.int32, (rows, rows), 0)
                across_cols = lax.broadcasted_iota(jnp.int32, (rows, rows), 1)
                chance = chance - jnp.where(across_rows == across_cols, 1.0, 0.0)
            weights = (scale * chance).astype(jnp.bfloat16)
            term = jnp.dot(weights, other, preferred_element_type=jnp.float32)
            acc[d] = term if on_diagonal else acc[d] + term

    pieces = (range(CHUNKS // 2), range(CHUNKS // 2, CHUNKS))

    def see(d, slot):
        for c in range(CHUNKS):
            arrived(d, slot, c)

    def land(slot):
        see(TEXT, slot)
        see(IMAGE, slot)

    def pass_on(d, slot, piece, side=None, wait=True):
        def run():
            for c in pieces[piece]:
                if wait:
                    arrived(d, slot, c)
                forward(d, slot, c)

        if side is None:
            run()
        else:
            pl.when(sides[d] == side)(run)

    def pass_both(slot, piece, side=None):
        pass_on(TEXT, slot, piece, side)
        pass_on(IMAGE, slot, piece, side)

    def handed(d, piece):
        pass_on(d, VIA, piece, NEAR)
        pass_on(d, 2, piece, FAR)

    def cross(d, piece):
        if d == IMAGE and piece == 0:
            pl.semaphore_wait(open_sem, 1)
        for c in pieces[piece]:
            arrived(d, VIA, c)
            copy(d, 11, VIA, COL + 2, c, at_col(signs[d] * (2 - depth))).start()

    def turn_back(piece):
        for c in pieces[piece]:
            copy(IMAGE, 0, jnp.where(sides[IMAGE] == 0, VIA, 2), COL + 1, c, turn).start()

    def finish(d):
        see(d, COL + 3)
        meet(COL + 3, (d,))
        inverse = inv[1 - d]
        unit = raw[1 - d].astype(jnp.float32) * inverse
        direction = acc[d]
        along = jnp.sum(unit * direction, axis=-1, keepdims=True)
        (img_out, txt_out)[d][...] = inverse * (direction - unit * along)

    meet(OWN, on_diagonal=True)

    @when(jnp.logical_not(top), jnp.logical_not(bottom))
    def _():
        for piece in range(2):
            pass_both(4, piece)
            pl.when(befores[TEXT])(functools.partial(cross, TEXT, piece))
            pass_both(COL + 1, piece)
            pass_both(2, piece, FAR)
            pl.when(befores[IMAGE])(functools.partial(cross, IMAGE, piece))
        meet(4)
        meet(COL + 1)
        for piece in range(2):
            pass_both(COL + 2, piece)
            pass_both(2, piece, NEAR)
            pass_both(6, piece, FAR)
        meet(COL + 2)
        meet(2)
        land(3)
        meet(3)
        pass_both(6, 0, NEAR)
        land(1)
        meet(1)
        pass_both(6, 1, NEAR)
        meet(6)
        for slot in (5, 7):
            land(slot)
            meet(slot)
        finish(TEXT)
        finish(IMAGE)

    @pl.when(bottom)
    def _():
        handed(IMAGE, 0)
        pass_both(4, 0)
        pl.semaphore_wait(open_sem, 2)
        turn_back(0)
        handed(IMAGE, 1)
        turn_back(1)
        pass_both(4, 1)
        meet(4)
        see(IMAGE, COL + 1)
        meet(COL + 1, (IMAGE,))
        pass_on(IMAGE, 2, 0, NEAR)
        pass_on(TEXT, 2, 0)
        pass_on(IMAGE, 6, 0, FAR)
        pass_on(TEXT, COL + 1, 0)
        pass_on(IMAGE, 2, 1, NEAR)
        pass_on(TEXT, 2, 1)
        pass_on(IMAGE, 6, 1, FAR)
        pass_on(TEXT, COL + 1, 1)
        meet(2)
        pass_on(TEXT, 6, 0)
        meet(COL + 1, (TEXT,))
        pass_on(TEXT, 6, 1)
        meet(6, (TEXT,))
        pass_on(IMAGE, COL + 2, 0)
        pass_on(IMAGE, COL + 2, 1)
        pass_on(IMAGE, 6, 0, NEAR)
        pass_on(TEXT, COL + 2, 0)
        land(3)
        meet(3)
        meet(COL + 2, (IMAGE,))
        pass_on(IMAGE, 6, 1, NEAR)
        meet(6, (IMAGE,))
        land(1)
        meet(1)
        pass_on(TEXT, COL + 2, 1)
        meet(COL + 2, (TEXT,))
        for slot in (5, 7):
            land(slot)
            meet(slot)
        finish(IMAGE)
        finish(TEXT)

    @pl.when(top)
    def _():
        for piece in range(2):
            handed(TEXT, piece)
            pass_both(4, piece)
        meet(4)
        see(TEXT, COL + 1)
        meet(COL + 1, (TEXT,))
        pass_on(IMAGE, COL + 1, 0)
        pass_on(IMAGE, COL + 1, 1)
        for piece in range(2):
            pass_on(TEXT, 2, piece, NEAR)
            pass_on(IMAGE, 2, piece)
            pass_on(TEXT, COL + 2, piece)
            pass_on(TEXT, 6, piece, FAR)
        meet(COL + 1, (IMAGE,))
        meet(2)
        meet(COL + 2, (TEXT,))
        pass_on(IMAGE, 6, 0)
        pass_on(IMAGE, COL + 2, 0)
        land(3)
        meet(3)
        pass_on(TEXT, 6, 0, NEAR)
        pass_on(IMAGE, 6, 1)
        pass_on(IMAGE, COL + 2, 1)
        land(1)
        meet(1)
        pass_on(TEXT, 6, 1, NEAR)
        meet(6)
        meet(COL + 2, (IMAGE,))
        for slot in (5, 7):
            land(slot)
            meet(slot)
        finish(TEXT)
        finish(IMAGE)

    for d in range(2):
        for number in range(12):
            for c in range(CHUNKS):

                def sent(d=d, number=number, c=c):
                    copy(d, number, OWN, 1, c, sibling).wait_send()

                handed = jnp.logical_and(lasts[d], sides[d] == 0)
                if number == 1:
                    pl.when(jnp.logical_not(lasts[d]))(sent)
                elif number == 10:
                    pl.when(jnp.logical_or(handed, befores[d]))(sent)
                elif number == 11:
                    pl.when(befores[d])(sent)
                else:
                    sent()


def on_device(n_row, n_col, picture, caption, scale_exponent, offset):
    rows, width = picture.shape
    scalar = pl.BlockSpec(memory_space=pltpu.SMEM)
    whole = pl.BlockSpec(memory_space=pltpu.HBM)
    out = jax.ShapeDtypeStruct((rows, width), jnp.float32)
    return pl.pallas_call(
        functools.partial(kernel, n_row, n_col),
        out_shape=(out, out),
        in_specs=[scalar, scalar, whole, whole],
        out_specs=[pl.BlockSpec(memory_space=pltpu.VMEM)] * 2,
        scratch_shapes=[
            pltpu.VMEM((2, rows, width), jnp.bfloat16),
            pltpu.VMEM((2, 12, rows, width), jnp.bfloat16),
            pltpu.VMEM((2, rows, width), jnp.float32),
            pltpu.VMEM((2, rows, 1), jnp.float32),
            pltpu.SemaphoreType.DMA((2, 12, CHUNKS)),
            pltpu.SemaphoreType.DMA((2, 12, CHUNKS)),
            pltpu.SemaphoreType.DMA((2, CHUNKS)),
            pltpu.SemaphoreType.REGULAR,
        ],
        compiler_params=pltpu.CompilerParams(
            collective_id=0, has_side_effects=True, vmem_limit_bytes=48 << 20
        ),
    )(
        scale_exponent.reshape(1, 1),
        offset.reshape(1, 1),
        pltpu.with_memory_space_constraint(caption, pltpu.HBM),
        pltpu.with_memory_space_constraint(picture, pltpu.HBM),
    )


def solution(mesh):
    return jax.shard_map(
        functools.partial(on_device, mesh.shape["row"], mesh.shape["col"]),
        mesh=mesh,
        in_specs=(P(("row", "col"), None), P(("row", "col"), None), P(), P()),
        out_specs=(P(("row", "col"), None), P(("row", "col"), None)),
        check_vma=False,
    )
```

```python
import functools

import jax
import jax.numpy as jnp
from jax import lax
from jax.experimental import pallas as pl
from jax.experimental.pallas import tpu as pltpu
from jax.sharding import PartitionSpec as P

MESH = pl.DeviceIdType.MESH
eps_norm = 1e-06

OWN, COL, VIA = 0, 7, 11
CHUNKS = 4
TEXT, IMAGE = 0, 1
NEAR, FAR = 0, 1


def kernel(
    n_row, n_col, scale_ref, bias_ref, txt_ref, img_ref, img_out, txt_out, raw, buf, acc, inv, send_sem, recv_sem, load_sem, open_sem
):
    rows, width = txt_ref.shape
    part = rows // CHUNKS
    row, col = lax.axis_index("row"), lax.axis_index("col")
    core = lax.rem(row, 2)
    half = lax.rem(row // 2, 2)
    depth = n_col // 2
    level = lax.rem(col, depth)
    top, bottom = level == depth - 1, level == 0

    def at(row_offset, col_offset):
        return (lax.rem(row + row_offset + n_row, n_row), lax.rem(col + col_offset + n_col, n_col))

    def at_row(offset):
        return at(offset, 0)

    def at_col(offset):
        return at(0, offset)

    beside = 2 - 4 * half
    sibling = at_row(1 - 2 * core)
    partner = at_row(beside)
    across = at_row(6 * core - 3)
    turn = at(beside, jnp.where(top, 1, -1))
    crossing = at_col(depth)
    befores = (level == depth - 2, level == 1)

    barrier = pltpu.get_barrier_semaphore()

    def greet(peer):
        pl.semaphore_signal(barrier, inc=1, device_id=peer, device_id_type=MESH)

    for peer in (at_row(4), at_row(-4), sibling, partner, across, at_col(-1)):
        greet(peer)

    @pl.when(jnp.logical_not(top))
    def _():
        greet(at_col(1))

    @pl.when(bottom)
    def _():
        greet(turn)

    @pl.when(level < 2)
    def _():
        greet(at_col(depth - 2))

    @pl.when(jnp.logical_or(*befores))
    def _():
        greet(crossing)

    def load(d, c):
        span = pl.ds(c * part, part)
        return pltpu.make_async_copy((txt_ref, img_ref)[d].at[span], raw.at[d, span], load_sem.at[d, c])

    for d in range(2):
        for c in range(CHUNKS):
            load(d, c).start()

    def normalise(d, c):
        load(d, c).wait()
        span = pl.ds(c * part, part)
        values = raw[d, span, :].astype(jnp.float32)
        inverse = lax.rsqrt(jnp.sum(values * values, axis=-1, keepdims=True) + eps_norm)
        inv[d, span, :] = inverse
        buf[d, OWN, span, :] = (values * inverse).astype(jnp.bfloat16)

    for c in range(CHUNKS):
        normalise(TEXT, c)

    pl.semaphore_wait(barrier, 7 + jnp.where(level >= depth - 2, 2, 0) + jnp.where(level == 1, 1, 0) - jnp.where(bottom, 1, 0))

    @pl.when(top)
    def _():
        for peer in (at_col(1), turn, at_col(2 - depth)):
            pl.semaphore_signal(open_sem, inc=1, device_id=peer, device_id_type=MESH)

    def copy(d, number, source, slot, c, target):
        span = pl.ds(c * part, part)
        return pltpu.make_async_remote_copy(
            src_ref=buf.at[d, source, span],
            dst_ref=buf.at[d, slot, span],
            send_sem=send_sem.at[d, number, c],
            recv_sem=recv_sem.at[d, slot, c],
            device_id=target,
            device_id_type=MESH,
        )

    def when(*conditions):
        return pl.when(functools.reduce(jnp.logical_and, conditions))

    signs = (1, -1)
    sides = (half, 1 - half)
    ends = (core, 1 - core)
    lasts = (top, bottom)

    def first_sends(d, c):
        copy(d, 3, OWN, 4, c, at_row(4 * signs[d])).start()

        @when(jnp.logical_not(lasts[d]), sides[d] == 0)
        def _():
            copy(d, 5, OWN, 2, c, partner).start()

        @when(jnp.logical_not(lasts[d]))
        def _():
            copy(d, 0, OWN, COL + 1, c, at_col(signs[d])).start()

        if d == IMAGE:

            @pl.when(befores[d])
            def _():
                copy(d, 10, OWN, VIA, c, crossing).start()

        @when(ends[d] == 0)
        def _():
            copy(d, 6, OWN, 1, c, sibling).start()

    def arrived(d, slot, c):
        copy(d, 0, OWN, slot, c, sibling).wait_recv()

    def forward(d, slot, c):
        sign, h, e, last = signs[d], sides[d], ends[d], lasts[d]
        if slot == COL + 1:

            @pl.when(jnp.logical_not(last))
            def _():
                copy(d, 1, slot, slot + 1, c, at_col(sign)).start()

        elif slot == COL + 2:
            copy(d, 2, slot, slot + 1, c, at_col(sign)).start()
        elif slot == VIA:
            if d == TEXT:
                copy(d, 0, VIA, COL + 1, c, turn).start()
            copy(d, 10, VIA, 2, c, at_row(4 * sign)).start()
        elif slot == 4:

            @when(h == 1, jnp.logical_not(last))
            def _():
                copy(d, 5, 4, 2, c, partner).start()

            @when(e == 1)
            def _():
                copy(d, 6, 4, 7, c, across).start()

            copy(d, 8, 4, 5 - 2 * e, c, sibling).start()
        elif slot == 2:
            if d == TEXT:

                @when(h == 1, last)
                def _():
                    copy(d, 0, 2, COL + 1, c, turn).start()

            copy(d, 4, 2, 6, c, at_row(4 * sign)).start()
            copy(d, 7, 2, 3 - 2 * e, c, sibling).start()
        elif slot == 6:
            copy(d, 9, 6, 7 - 2 * e, c, sibling).start()

    def hand_over(d):
        @pl.when(lasts[d])
        def _():
            for c in range(CHUNKS):
                copy(d, 5, OWN, jnp.where(sides[d] == 0, 2, VIA), c, partner).start()

    hand_over(TEXT)

    @pl.when(befores[TEXT])
    def _():
        for c in range(CHUNKS):
            copy(TEXT, 10, OWN, VIA, c, crossing).start()

    @pl.when(top)
    def _():
        for c in range(CHUNKS):
            first_sends(TEXT, c)

    for c in range(CHUNKS):
        normalise(IMAGE, c)
    hand_over(IMAGE)
    for c in range(CHUNKS):

        @pl.when(jnp.logical_not(top))
        def _(c=c):
            first_sends(TEXT, c)

        first_sends(IMAGE, c)

    scale = jnp.exp(jnp.full((1, rows), scale_ref[0, 0], jnp.float32))
    bias = bias_ref[0, 0]

    def meet(slot, directions=(TEXT, IMAGE), on_diagonal=False):
        for d in directions:
            other = buf[d, slot]
            cosines = lax.dot_general(
                buf[1 - d, OWN], other, (((1,), (1,)), ((), ())), preferred_element_type=jnp.float32
            )
            chance = jax.nn.sigmoid(scale * cosines + bias)
            if on_diagonal:
                across_rows = lax.broadcasted_iota(jnp.int32, (rows, rows), 0)
                across_cols = lax.broadcasted_iota(jnp.int32, (rows, rows), 1)
                chance = chance - jnp.where(across_rows == across_cols, 1.0, 0.0)
            weights = (scale * chance).astype(jnp.bfloat16)
            term = jnp.dot(weights, other, preferred_element_type=jnp.float32)
            acc[d] = term if on_diagonal else acc[d] + term

    pieces = (range(CHUNKS // 2), range(CHUNKS // 2, CHUNKS))

    def see(d, slot):
        for c in range(CHUNKS):
            arrived(d, slot, c)

    def land(slot):
        see(TEXT, slot)
        see(IMAGE, slot)

    def pass_on(d, slot, piece, side=None, wait=True):
        def run():
            for c in pieces[piece]:
                if wait:
                    arrived(d, slot, c)
                forward(d, slot, c)

        if side is None:
            run()
        else:
            pl.when(sides[d] == side)(run)

    def pass_both(slot, piece, side=None):
        pass_on(TEXT, slot, piece, side)
        pass_on(IMAGE, slot, piece, side)

    def handed(d, piece):
        pass_on(d, VIA, piece, NEAR)
        pass_on(d, 2, piece, FAR)

    def cross(d, piece):
        if d == IMAGE and piece == 0:
            pl.semaphore_wait(open_sem, 1)
        for c in pieces[piece]:
            arrived(d, VIA, c)
            copy(d, 11, VIA, COL + 2, c, at_col(signs[d] * (2 - depth))).start()

    def turn_back(piece):
        for c in pieces[piece]:
            copy(IMAGE, 0, jnp.where(sides[IMAGE] == 0, VIA, 2), COL + 1, c, turn).start()

    def finish(d):
        see(d, COL + 3)
        meet(COL + 3, (d,))
        inverse = inv[1 - d]
        unit = raw[1 - d].astype(jnp.float32) * inverse
        direction = acc[d]
        along = jnp.sum(unit * direction, axis=-1, keepdims=True)
        (img_out, txt_out)[d][...] = inverse * (direction - unit * along)

    meet(OWN, on_diagonal=True)

    @when(jnp.logical_not(top), jnp.logical_not(bottom))
    def _():
        for piece in range(2):
            pass_both(4, piece)
            pl.when(befores[TEXT])(functools.partial(cross, TEXT, piece))
            pass_both(COL + 1, piece)
            pass_both(2, piece, FAR)
            pl.when(befores[IMAGE])(functools.partial(cross, IMAGE, piece))
        meet(4)
        meet(COL + 1)
        for piece in range(2):
            pass_both(COL + 2, piece)
            pass_both(2, piece, NEAR)
            pass_both(6, piece, FAR)
        meet(COL + 2)
        meet(2)
        land(3)
        meet(3)
        pass_both(6, 0, NEAR)
        land(1)
        meet(1)
        pass_both(6, 1, NEAR)
        meet(6)
        for slot in (5, 7):
            land(slot)
            meet(slot)
        finish(TEXT)
        finish(IMAGE)

    @pl.when(bottom)
    def _():
        handed(IMAGE, 0)
        pass_both(4, 0)
        pl.semaphore_wait(open_sem, 2)
        turn_back(0)
        handed(IMAGE, 1)
        turn_back(1)
        pass_both(4, 1)
        meet(4)
        see(IMAGE, COL + 1)
        meet(COL + 1, (IMAGE,))
        pass_on(IMAGE, 2, 0, NEAR)
        pass_on(TEXT, 2, 0)
        pass_on(IMAGE, 6, 0, FAR)
        pass_on(TEXT, COL + 1, 0)
        pass_on(IMAGE, 2, 1, NEAR)
        pass_on(TEXT, 2, 1)
        pass_on(IMAGE, 6, 1, FAR)
        pass_on(TEXT, COL + 1, 1)
        meet(2)
        pass_on(TEXT, 6, 0)
        meet(COL + 1, (TEXT,))
        pass_on(TEXT, 6, 1)
        meet(6, (TEXT,))
        pass_on(IMAGE, COL + 2, 0)
        pass_on(IMAGE, COL + 2, 1)
        pass_on(IMAGE, 6, 0, NEAR)
        pass_on(TEXT, COL + 2, 0)
        land(3)
        meet(3)
        meet(COL + 2, (IMAGE,))
        pass_on(IMAGE, 6, 1, NEAR)
        meet(6, (IMAGE,))
        land(1)
        meet(1)
        pass_on(TEXT, COL + 2, 1)
        meet(COL + 2, (TEXT,))
        for slot in (5, 7):
            land(slot)
            meet(slot)
        finish(IMAGE)
        finish(TEXT)

    @pl.when(top)
    def _():
        for piece in range(2):
            handed(TEXT, piece)
            pass_both(4, piece)
        meet(4)
        see(TEXT, COL + 1)
        meet(COL + 1, (TEXT,))
        pass_on(IMAGE, COL + 1, 0)
        pass_on(IMAGE, COL + 1, 1)
        for piece in range(2):
            pass_on(TEXT, 2, piece, NEAR)
            pass_on(TEXT, COL + 2, piece)
            pass_on(IMAGE, 2, piece)
            pass_on(TEXT, 6, piece, FAR)
        meet(COL + 1, (IMAGE,))
        meet(2)
        meet(COL + 2, (TEXT,))
        pass_on(IMAGE, 6, 0)
        pass_on(IMAGE, COL + 2, 0)
        land(3)
        meet(3)
        pass_on(TEXT, 6, 0, NEAR)
        pass_on(IMAGE, 6, 1)
        pass_on(IMAGE, COL + 2, 1)
        land(1)
        meet(1)
        pass_on(TEXT, 6, 1, NEAR)
        meet(6)
        meet(COL + 2, (IMAGE,))
        for slot in (5, 7):
            land(slot)
            meet(slot)
        finish(TEXT)
        finish(IMAGE)

    for d in range(2):
        for number in range(12):
            for c in range(CHUNKS):

                def sent(d=d, number=number, c=c):
                    copy(d, number, OWN, 1, c, sibling).wait_send()

                handed = jnp.logical_and(lasts[d], sides[d] == 0)
                if number == 1:
                    pl.when(jnp.logical_not(lasts[d]))(sent)
                elif number == 10:
                    pl.when(jnp.logical_or(handed, befores[d]))(sent)
                elif number == 11:
                    pl.when(befores[d])(sent)
                else:
                    sent()


def on_device(n_row, n_col, picture, caption, scale_exponent, offset):
    rows, width = picture.shape
    scalar = pl.BlockSpec(memory_space=pltpu.SMEM)
    whole = pl.BlockSpec(memory_space=pltpu.HBM)
    out = jax.ShapeDtypeStruct((rows, width), jnp.float32)
    return pl.pallas_call(
        functools.partial(kernel, n_row, n_col),
        out_shape=(out, out),
        in_specs=[scalar, scalar, whole, whole],
        out_specs=[pl.BlockSpec(memory_space=pltpu.VMEM)] * 2,
        scratch_shapes=[
            pltpu.VMEM((2, rows, width), jnp.bfloat16),
            pltpu.VMEM((2, 12, rows, width), jnp.bfloat16),
            pltpu.VMEM((2, rows, width), jnp.float32),
            pltpu.VMEM((2, rows, 1), jnp.float32),
            pltpu.SemaphoreType.DMA((2, 12, CHUNKS)),
            pltpu.SemaphoreType.DMA((2, 12, CHUNKS)),
            pltpu.SemaphoreType.DMA((2, CHUNKS)),
            pltpu.SemaphoreType.REGULAR,
        ],
        compiler_params=pltpu.CompilerParams(
            collective_id=0, has_side_effects=True, vmem_limit_bytes=48 << 20
        ),
    )(
        scale_exponent.reshape(1, 1),
        offset.reshape(1, 1),
        pltpu.with_memory_space_constraint(caption, pltpu.HBM),
        pltpu.with_memory_space_constraint(picture, pltpu.HBM),
    )


def solution(mesh):
    return jax.shard_map(
        functools.partial(on_device, mesh.shape["row"], mesh.shape["col"]),
        mesh=mesh,
        in_specs=(P(("row", "col"), None), P(("row", "col"), None), P(), P()),
        out_specs=(P(("row", "col"), None), P(("row", "col"), None)),
        check_vma=False,
    )
```
